256 devices in a mesh: seq: 64 (over x, y_hi, z), head: 4 (over y_lo, core).
Axes of the slice: x: 4, y: 4 (y_hi: 2, y_lo: 2; y = y_hi * 2 + y_lo), z: 8, core: 2. Of those that a mesh axis runs over, the one named last changes fastest.
Arguments:
- queries: bfloat16 [131072, 2048], P('seq', 'head'), may hold values from -6 to 6
- keys: bfloat16 [131072, 2048], P('seq', 'head'), may hold values from -6 to 6
- values: bfloat16 [131072, 2048], P('seq', 'head'), may hold values from -6 to 6
- out_weight: bfloat16 [2048, 2048], P('head'), may hold values from -0.125 to 0.125
Outputs:
- mixed: bfloat16 [131072, 2048], P(('seq', 'head'))
The draws below stay inside these ranges and needn't reach their ends.
All inputs are finite; a program needn't handle non-finite values.
Results may differ from the reference program's by a relative error of at most 0.0051.
Values may be sent and summed in bfloat16 or wider, within the bound.
No kernel may reach another device: no remote copies, remote signals or barrier semaphores. Data moves between devices by JAX's collectives and lax.ppermute only.
A program may use at most 128 MiB of HBM per device.

```python
import jax
import jax.numpy as jnp
from jax import lax

HEADS = 16
HD = 128
D = 2048
TOKENS = 131072


def regional(key, spread):
    columns = HEADS * HD
    coarse_three = jax.random.normal(jax.random.fold_in(key, 11), (TOKENS // 4096, columns), jnp.float32) * spread
    coarse_two = jax.random.normal(jax.random.fold_in(key, 12), (TOKENS // 256, columns), jnp.float32) * spread
    coarse_one = jax.random.normal(jax.random.fold_in(key, 13), (TOKENS // 16, columns), jnp.float32) * spread
    return jnp.repeat(coarse_three, 4096, axis=0) + jnp.repeat(coarse_two, 256, axis=0) + jnp.repeat(coarse_one, 16, axis=0)


def draw_queries(key, part):
    key = jax.random.fold_in(key, 1)
    result = jnp.clip(jax.random.normal(key, (TOKENS, HEADS * HD), jnp.float32), -6.0, 6.0)
    return result.astype(jnp.bfloat16)


def draw_keys(key, part):
    key = jax.random.fold_in(key, 2)
    base = jax.random.normal(key, (TOKENS, HEADS * HD), jnp.float32) * 0.8 + regional(jax.random.fold_in(key, 5), 0.6)
    result = jnp.clip(base, -6.0, 6.0)
    return result.astype(jnp.bfloat16)


def draw_values(key, part):
    key = jax.random.fold_in(key, 3)
    base = jax.random.normal(key, (TOKENS, HEADS * HD), jnp.float32) * 0.8 + regional(jax.random.fold_in(key, 5), 0.6)
    return jnp.clip(base, -6.0, 6.0).astype(jnp.bfloat16)


def block_scale(own_key, dims, shards, low, largest):
    level, own = 1.0, jax.random.fold_in(own_key, 6)
    for axis_at, parts in shards:
        draws = jnp.exp(jax.random.uniform(jax.random.fold_in(own, axis_at), (parts,), jnp.float32, low / len(shards), largest / len(shards)))
        level = level * jnp.repeat(draws, dims[axis_at] // parts).reshape([-1 if axis == axis_at else 1 for axis in range(len(dims))])
    return level


def scatter_about(key, shape, deviation, reach, pieces=(), held_as=jnp.bfloat16):
    entries = deviation * jax.random.normal(key, shape, jnp.float32)
    if pieces:
        entries = entries * block_scale(key, shape, pieces, -0.22, 0.18)
    return jnp.clip(entries, -reach, reach).astype(held_as)


def setup_inputs(seed: int = 0) -> dict:
    splits = jax.random.split(jax.random.key(seed), 5)
    return {
        "queries": draw_queries(jax.random.fold_in(splits[4], 71), 0),
        "keys": draw_keys(jax.random.fold_in(splits[4], 71), 0),
        "values": draw_values(jax.random.fold_in(splits[4], 71), 0),
        "out_weight": scatter_about(splits[3], (D, D), D ** -0.5, 0.125, ((0, 4),)),
    }


def pooled(stack, size):
    shaped = stack.astype(jnp.float32).reshape(stack.shape[0], -1, size, stack.shape[2])
    return jnp.mean(shaped, axis=2).astype(jnp.bfloat16)


def attend_block(query_block, start, fine_window, coarse_window, middle_window, summit, total):
    rows = query_block.shape[0]
    width = query_block.shape[1]
    heads = width // HD
    positions = start + jnp.arange(rows, dtype=jnp.int32)
    fine_block = positions // 16
    first_level = positions // 256
    second_level = positions // 4096
    near_tokens = start - 16 + jnp.arange(rows + 32, dtype=jnp.int32)
    near_mask = (jnp.abs(near_tokens[None, :] // 16 - fine_block[:, None]) <= 1) & (near_tokens[None, :] >= 0) & (near_tokens[None, :] < total)
    level_one = start // 16 - 16 + jnp.arange(rows // 16 + 32, dtype=jnp.int32)
    one_mask = (jnp.abs(level_one[None, :] // 16 - first_level[:, None]) <= 1) & (jnp.abs(level_one[None, :] - fine_block[:, None]) > 1) & (level_one[None, :] >= 0) & (level_one[None, :] < total // 16)
    level_two = 16 * (start // 4096) - 16 + jnp.arange(48, dtype=jnp.int32)
    two_mask = (jnp.abs(level_two[None, :] // 16 - second_level[:, None]) <= 1) & (jnp.abs(level_two[None, :] - first_level[:, None]) > 1) & (level_two[None, :] >= 0) & (level_two[None, :] < total // 256)
    level_three = jnp.arange(summit.shape[1], dtype=jnp.int32)
    three_mask = jnp.abs(level_three[None, :] - second_level[:, None]) > 1
    mask = jnp.concatenate([near_mask, one_mask, two_mask, three_mask], axis=1)
    key_rows = jnp.concatenate([fine_window[0], coarse_window[0], middle_window[0], summit[0]], axis=0).reshape(-1, heads, HD)
    value_rows = jnp.concatenate([fine_window[1], coarse_window[1], middle_window[1], summit[1]], axis=0).reshape(-1, heads, HD)
    query_heads = query_block.reshape(rows, heads, HD)
    scores = jnp.einsum('rhd,khd->hrk', query_heads.astype(jnp.float32), key_rows.astype(jnp.float32), precision=lax.Precision.HIGHEST) * (HD ** -0.5)
    scores = jnp.where(mask[None], scores, -jnp.inf)
    peak = jnp.max(scores, axis=2, keepdims=True)
    expo = jnp.where(mask[None], jnp.exp(scores - peak), 0.0)
    totals = jnp.sum(expo, axis=2)
    weights = expo.astype(jnp.bfloat16)
    summed = jnp.einsum('hrk,khd->rhd', weights.astype(jnp.float32), value_rows.astype(jnp.float32), precision=lax.Precision.HIGHEST)
    return (summed / jnp.transpose(totals)[:, :, None]).astype(jnp.bfloat16).reshape(rows, width)


def reference(queries, keys, values, out_weight):
    stack = jnp.stack([keys, values])
    padding = ((0, 0), (16, 16), (0, 0))
    fine_pad = jnp.pad(stack, padding)
    coarse_pad = jnp.pad(pooled(stack, 16), padding)
    middle = pooled(stack, 256)
    summit = pooled(middle, 16)
    middle_pad = jnp.pad(middle, padding)

    def one_block(index):
        start = index * 512
        query_block = lax.dynamic_slice_in_dim(queries, start, 512, 0)
        fine_window = lax.dynamic_slice_in_dim(fine_pad, start, 544, 1)
        coarse_window = lax.dynamic_slice_in_dim(coarse_pad, start // 16, 64, 1)
        middle_window = lax.dynamic_slice_in_dim(middle_pad, 16 * (start // 4096), 48, 1)
        return attend_block(query_block, start, fine_window, coarse_window, middle_window, summit, TOKENS)

    attended = lax.map(one_block, jnp.arange(TOKENS // 512, dtype=jnp.int32)).reshape(TOKENS, -1)
    return jnp.dot(attended, out_weight, preferred_element_type=jnp.float32).astype(jnp.bfloat16)
```

```python
import functools

import jax
import jax.numpy as jnp
from jax import lax
from jax.experimental import pallas as pl
from jax.experimental.pallas import tpu as pltpu
from jax.sharding import PartitionSpec as P

HD = 128
HEADS = 4
WIDE = HEADS * HD
LOG2E = 1.4426950408889634
SCORE = HD**-0.5 * LOG2E
NEG = -1e30
F32 = jnp.float32
BF16 = jnp.bfloat16
VMEM_LIMIT = 48 * 1024 * 1024

TK, TV, AK, AV, BK, BV = (16 * i for i in range(6))


def mean_rows(count, size, scale):
    rows = lax.broadcasted_iota(jnp.int32, (count, count * size), 0)
    cols = lax.broadcasted_iota(jnp.int32, (count, count * size), 1)
    return jnp.where(rows == cols // size, scale, 0.0).astype(BF16)


def pool_kernel(info, k_ref, v_ref, l1_ref, near_ref, far_ref, sums):
    step = pl.program_id(0)
    odd = info[0] % 2
    ones = mean_rows(16, 16, 1.0)
    for which, ref in ((0, k_ref), (1, v_ref)):
        for part in range(2):
            block = ref[256 * part : 256 * (part + 1), :]
            total = jnp.dot(ones, block, preferred_element_type=F32)
            at = pl.multiple_of(32 * step + 16 * part, 16)
            sums[which, pl.ds(at, 16), :] = total
            l1_ref[which, 16 * part : 16 * (part + 1), :] = (total * 0.0625).astype(BF16)

    @pl.when(step == 0)
    def _():
        low = (k_ref[0:16, :], v_ref[0:16, :], l1_ref[0, 0:16, :], l1_ref[1, 0:16, :])
        for at, rows in enumerate(low):
            rows = rows.astype(BF16)

            @pl.when(odd == 1)
            def _():
                near_ref[16 * at : 16 * at + 16, :] = rows

            @pl.when(odd == 0)
            def _():
                far_ref[16 * at : 16 * at + 16, :] = rows

    @pl.when(step == pl.num_programs(0) - 1)
    def _():
        high = (k_ref[496:512, :], v_ref[496:512, :], l1_ref[0, 16:32, :], l1_ref[1, 16:32, :])
        for at, rows in enumerate(high):

            @pl.when(odd == 0)
            def _():
                near_ref[16 * at : 16 * at + 16, :] = rows

            @pl.when(odd == 1)
            def _():
                far_ref[16 * at : 16 * at + 16, :] = rows

        for which, at in ((0, BK), (1, BV)):
            means = jnp.sum(sums[which].reshape(8, 16, WIDE), axis=1) * (1.0 / 256.0)
            both = jnp.concatenate([means, means], axis=0)
            row = lax.broadcasted_iota(jnp.int32, (16, WIDE), 0)
            near_ref[at : at + 16, :] = jnp.where(row // 8 == odd, both, 0.0).astype(BF16)


def pool(info, keys, values):
    rows = keys.shape[0]
    steps = rows // 512
    return pl.pallas_call(
        pool_kernel,
        grid_spec=pltpu.PrefetchScalarGridSpec(
            num_scalar_prefetch=1,
            grid=(steps,),
            in_specs=[pl.BlockSpec((512, WIDE), lambda i, s: (i, 0))] * 2,
            out_specs=[
                pl.BlockSpec((2, 32, WIDE), lambda i, s: (0, i, 0)),
                pl.BlockSpec((96, WIDE), lambda i, s: (0, 0)),
                pl.BlockSpec((64, WIDE), lambda i, s: (0, 0)),
            ],
            scratch_shapes=[pltpu.VMEM((2, rows // 16, WIDE), F32)],
        ),
        out_shape=[
            jax.ShapeDtypeStruct((2, rows // 16, WIDE), BF16),
            jax.ShapeDtypeStruct((96, WIDE), BF16),
            jax.ShapeDtypeStruct((64, WIDE), BF16),
        ],
        cost_estimate=pl.CostEstimate(
            flops=4 * rows * 16 * WIDE, bytes_accessed=4 * rows * WIDE, transcendentals=0
        ),
        compiler_params=pltpu.CompilerParams(vmem_limit_bytes=VMEM_LIMIT),
        name="pool",
    )(info, keys, values)


def attend_kernel(
    total, info, q_ref, k_ref, kp_ref, kn_ref, v_ref, vp_ref, vn_ref, l1_ref, mid_ref, near_ref,
    far_ref, farther_ref, l3_ref, out_ref, kx, vx, l1x, sk, sv,
):
    step = pl.program_id(0)
    block = info[0]
    group = info[1 + step]
    odd = block % 2
    last_group = 2048 // 256 - 1

    @pl.when(step == 0)
    def _():
        for which, at in ((0, AK), (1, AV)):
            near, far = near_ref[at : at + 16, :], far_ref[at : at + 16, :]
            l1x[which, 0:16, :] = jnp.where(odd == 1, near, far)
            l1x[which, 16:144, :] = l1_ref[which]
            l1x[which, 144:160, :] = jnp.where(odd == 1, far, near)
        for scratch, at, which in ((sk, BK, 0), (sv, BV, 1)):
            scratch[48:64, :] = mid_ref[at - BK : at - BK + 16, :]
            scratch[64:80, :] = far_ref[at : at + 16, :]
            scratch[80:96, :] = farther_ref[at - BK : at - BK + 16, :]
            scratch[96:128, :] = l3_ref[which]
        zeros = jnp.zeros((32, WIDE), BF16)
        kx[288:320, :] = zeros
        vx[288:320, :] = zeros

    for scratch, main, before, after, at in (
        (kx, k_ref, kp_ref, kn_ref, TK),
        (vx, v_ref, vp_ref, vn_ref, TV),
    ):
        near, far = near_ref[at : at + 16, :], far_ref[at : at + 16, :]
        low = jnp.where(odd == 1, near, far)
        high = jnp.where(odd == 1, far, near)
        scratch[0:16, :] = jnp.where(group == 0, low, before[...])
        scratch[16:272, :] = main[...]
        scratch[272:288, :] = jnp.where(group == last_group, high, after[...])
    window = pl.ds(pl.multiple_of(16 * group, 16), 48)
    sk[0:48, :] = l1x[0, window, :]
    sv[0:48, :] = l1x[1, window, :]

    c = 8 * block + group
    e = block // 2
    col = lax.broadcasted_iota(jnp.int32, (64, 128), 1)
    fine = lax.broadcasted_iota(jnp.int32, (64, 128), 0) // 16
    tile = col // 16
    beside = jnp.where(odd == 0, e - 1, e + 1)
    across = jnp.where(odd == 0, e + 1, e - 1)
    m = 16 * jnp.where(tile == 3, e, jnp.where(tile == 4, beside, across)) + col % 16
    term2 = jnp.where((m >= 0) & (m < total // 256) & (jnp.abs(m - c) > 1), 0.0, NEG)
    term3 = jnp.where(jnp.abs(col - 96 - e) > 1, 0.0, NEG)
    j = 16 * (c - 1) + col
    term1 = jnp.where((j >= 0) & (j < total // 16), 0.0, NEG)
    shared = jnp.where(col < 48, term1, jnp.where(col < 96, term2, term3))
    for part in range(4):
        token = 256 * c + 64 * part - 16 + col
        ok = (jnp.abs(tile - 1 - fine) <= 1) & (token >= 0) & (token < total)
        own = (col < 48) & (jnp.abs(col - 16 - 4 * part - fine) <= 1)
        bias = jnp.concatenate(
            [jnp.where(ok, 0.0, NEG), jnp.where(own, NEG, shared)], axis=1
        ).astype(F32)
        rows = slice(64 * part, 64 * part + 64)
        near_rows = slice(64 * part, 64 * part + 128)
        for head in range(HEADS):
            cols = slice(HD * head, HD * head + HD)
            key_rows = jnp.concatenate([kx[near_rows, cols], sk[:, cols]], axis=0)
            value_rows = jnp.concatenate([vx[near_rows, cols], sv[:, cols]], axis=0)
            scores = lax.dot_general(
                q_ref[rows, cols], key_rows, (((1,), (1,)), ((), ())), preferred_element_type=F32
            )
            scores = scores * SCORE + bias
            peak = jnp.max(scores, axis=1, keepdims=True)
            expo = jnp.exp2(scores - peak)
            sums = jnp.sum(expo, axis=1, keepdims=True)
            summed = jnp.dot(expo.astype(BF16), value_rows, preferred_element_type=F32)
            out_ref[rows, cols] = (summed / sums).astype(BF16)


def attend(total, info, queries, keys, values, l1, mid, near, far, farther, l3):
    def main(i, s):
        return (s[1 + i], 0)

    def before(i, s):
        return (jnp.maximum(16 * s[1 + i] - 1, 0), 0)

    def after(i, s):
        return (jnp.minimum(16 * s[1 + i] + 16, 127), 0)

    def whole(array):
        return pl.BlockSpec(array.shape, lambda i, s: (0,) * array.ndim)

    wide, thin_low, thin_high = (
        pl.BlockSpec((256, WIDE), main),
        pl.BlockSpec((16, WIDE), before),
        pl.BlockSpec((16, WIDE), after),
    )
    small = (l1, mid, near, far, farther, l3)
    return pl.pallas_call(
        functools.partial(attend_kernel, total),
        grid_spec=pltpu.PrefetchScalarGridSpec(
            num_scalar_prefetch=1,
            grid=(2,),
            in_specs=[wide, wide, thin_low, thin_high, wide, thin_low, thin_high]
            + [whole(array) for array in small],
            out_specs=pl.BlockSpec((256, WIDE), lambda i, s: (i, 0)),
            scratch_shapes=[
                pltpu.VMEM((320, WIDE), BF16),
                pltpu.VMEM((320, WIDE), BF16),
                pltpu.VMEM((2, 160, WIDE), BF16),
                pltpu.VMEM((128, WIDE), BF16),
                pltpu.VMEM((128, WIDE), BF16),
            ],
        ),
        out_shape=jax.ShapeDtypeStruct((512, WIDE), BF16),
        cost_estimate=pl.CostEstimate(
            flops=4 * 512 * 256 * WIDE, bytes_accessed=8 * 512 * WIDE, transcendentals=512 * 256 * HEADS
        ),
        compiler_params=pltpu.CompilerParams(vmem_limit_bytes=VMEM_LIMIT),
        name="attend",
    )(info, queries, keys, keys, keys, values, values, values, *small)


def project_kernel(info, a0, a1, a2, a3, w0, w1, w2y, w2z, w3y, w3z, out_ref):
    first = pl.multiple_of(256 * info[0], 256)
    second = pl.multiple_of(256 - 256 * info[0], 256)
    total = jnp.dot(a0[...], w0[...], preferred_element_type=F32)
    total += jnp.dot(a1[...], w1[...], preferred_element_type=F32)
    for a, y, z in ((a2, w2y, w2z), (a3, w3y, w3z)):
        total += jnp.dot(a[:, pl.ds(first, 256)], y[...], preferred_element_type=F32)
        total += jnp.dot(a[:, pl.ds(second, 256)], z[...], preferred_element_type=F32)
    out_ref[...] = total.astype(BF16)


def project(info, attended, weights):
    rows, columns = attended[0].shape[0], weights[0].shape[1]
    tile = 512
    return pl.pallas_call(
        project_kernel,
        grid_spec=pltpu.PrefetchScalarGridSpec(
            num_scalar_prefetch=1,
            grid=(columns // tile,),
            in_specs=[pl.BlockSpec(a.shape, lambda i, s: (0, 0)) for a in attended]
            + [pl.BlockSpec((w.shape[0], tile), lambda i, s: (0, i)) for w in weights],
            out_specs=pl.BlockSpec((rows, tile), lambda i, s: (0, i)),
        ),
        out_shape=jax.ShapeDtypeStruct((rows, columns), BF16),
        cost_estimate=pl.CostEstimate(
            flops=2 * rows * 2048 * columns, bytes_accessed=2 * 2048 * columns, transcendentals=0
        ),
        compiler_params=pltpu.CompilerParams(vmem_limit_bytes=VMEM_LIMIT),
        name="project",
    )(info, *attended, *weights)


def body(queries, keys, values, out_weight):
    blocks = lax.axis_size("seq")
    total = queries.shape[0] * blocks
    s = lax.axis_index("seq")
    h = lax.axis_index("head")
    half = (s // 16) % 2

    def permute(array, move):
        return lax.ppermute(array, "seq", [(i, move(i) % blocks) for i in range(blocks)])

    def swap(array, bit):
        return lax.ppermute(array, "head", [(i, i ^ bit) for i in range(4)])

    w_far_y = swap(lax.dynamic_slice_in_dim(out_weight, 256 * half, 256, 0), 2)
    w_near = swap(out_weight, 1)

    l1, to_near, to_far = pool(jnp.stack([s]).astype(jnp.int32), keys, values)
    near = permute(to_near, lambda i: i ^ 1)
    mid = to_near[BK:, :] + near[BK:, :]
    far = permute(jnp.concatenate([to_far, mid]), lambda i: i + 1 if i % 2 else i - 1)
    farther = permute(far[BK:, :], lambda i: i ^ 1)
    l3 = jnp.mean(mid.reshape(2, 16, WIDE).astype(F32), axis=1).astype(BF16)
    groups = [[2 * i + parity for i in range(blocks // 2)] for parity in range(2)]
    l3 = lax.all_to_all(
        jnp.broadcast_to(l3[None], (blocks // 2, 2, WIDE)), "seq", 0, 0, axis_index_groups=groups
    )
    l3 = jnp.swapaxes(l3, 0, 1)

    w_far_z = permute(w_far_y, lambda i: i ^ 16)
    w_cross_y = swap(w_far_y, 1)
    w_cross_z = swap(w_far_z, 1)

    outs = {}
    for bit in (2, 3, 1, 0):
        dest = h ^ bit
        info = jnp.stack([s, 2 * dest, 2 * dest + 1]).astype(jnp.int32)
        part = attend(total, info, queries, keys, values, l1, mid, near, far, farther, l3)
        outs[bit] = swap(part, bit) if bit else part

    return project(
        jnp.stack([half]).astype(jnp.int32),
        [outs[0], outs[1], outs[2], outs[3]],
        [out_weight, w_near, w_far_y, w_far_z, w_cross_y, w_cross_z],
    )


def solution(mesh):
    placed = (P("seq", "head"), P("seq", "head"), P("seq", "head"), P("head", None))
    return jax.shard_map(
        body, mesh=mesh, in_specs=placed, out_specs=P(("seq", "head"), None), check_vma=False
    )
```

```python
import functools

import jax
import jax.numpy as jnp
from jax import lax
from jax.experimental import pallas as pl
from jax.experimental.pallas import tpu as pltpu
from jax.sharding import PartitionSpec as P

HD = 128
HEADS = 4
WIDE = HEADS * HD
LOG2E = 1.4426950408889634
SCORE = HD**-0.5 * LOG2E
NEG = -1e30
F32 = jnp.float32
BF16 = jnp.bfloat16
POOL_VMEM, ATTEND_VMEM, PROJECT_VMEM = (mib * 1024 * 1024 for mib in (51, 51, 24))
CHUNKS = 4
ORDER = ((0, 2), (1, 1), (2, 3), (3, 0))
SMALL = pl.CostEstimate(flops=1000, bytes_accessed=1000, transcendentals=0)

TK, TV, AK, AV, BK, BV = (16 * i for i in range(6))


def mean_rows(count, size, scale):
    rows = lax.broadcasted_iota(jnp.int32, (count, count * size), 0)
    cols = lax.broadcasted_iota(jnp.int32, (count, count * size), 1)
    return jnp.where(rows == cols // size, scale, 0.0).astype(BF16)


def pool_kernel(k_hbm, v_hbm, l1_ref, near_ref, far_ref, k_ref, v_ref, sems):
    odd = lax.axis_index("seq") % 2
    ones = mean_rows(16, 16, 1.0)
    chunk = k_ref.shape[0] // CHUNKS
    copies = []
    for i in range(CHUNKS):
        rows = pl.ds(chunk * i, chunk)
        for which, (hbm, ref) in enumerate(((k_hbm, k_ref), (v_hbm, v_ref))):
            copy = pltpu.make_async_copy(hbm.at[rows, :], ref.at[rows, :], sems.at[which, i])
            copy.start()
            copies.append(copy)
    level2 = [[], []]
    for i in range(CHUNKS):
        for which, ref in enumerate((k_ref, v_ref)):
            copies[2 * i + which].wait()
            for at in range(chunk * i, chunk * (i + 1), 256):
                total = jnp.dot(ones, ref[at : at + 256, :], preferred_element_type=F32)
                l1_ref[which, at // 16 : at // 16 + 16, :] = (total * 0.0625).astype(BF16)
                level2[which].append(jnp.sum(total, axis=0, keepdims=True) * (1.0 / 256.0))

    last = k_ref.shape[0]
    low = [k_ref[0:16, :], v_ref[0:16, :], l1_ref[0, 0:16, :], l1_ref[1, 0:16, :]]
    high = [k_ref[last - 16 : last, :], v_ref[last - 16 : last, :]]
    high += [l1_ref[which, last // 16 - 16 : last // 16, :] for which in range(2)]
    for at, (below, above) in enumerate(zip(low, high)):
        rows = slice(16 * at, 16 * at + 16)
        near_ref[rows, :] = jnp.where(odd == 1, below, above)
        far_ref[rows, :] = jnp.where(odd == 1, above, below)
    row = lax.broadcasted_iota(jnp.int32, (16, WIDE), 0)
    for which, at in ((0, BK), (1, BV)):
        both = jnp.concatenate(level2[which] * 2, axis=0)
        near_ref[at : at + 16, :] = jnp.where(row // 8 == odd, both, 0.0).astype(BF16)


def pool(keys, values):
    rows = keys.shape[0]
    return pl.pallas_call(
        pool_kernel,
        in_specs=[
            pl.BlockSpec(memory_space=pltpu.HBM),
            pl.BlockSpec(memory_space=pltpu.HBM),
        ],
        out_specs=[pl.BlockSpec(memory_space=pltpu.VMEM)] * 3,
        scratch_shapes=[
            pltpu.VMEM((rows, WIDE), BF16),
            pltpu.VMEM((rows, WIDE), BF16),
            pltpu.SemaphoreType.DMA((2, CHUNKS)),
        ],
        out_shape=[
            jax.ShapeDtypeStruct((2, rows // 16, WIDE), BF16),
            jax.ShapeDtypeStruct((96, WIDE), BF16),
            jax.ShapeDtypeStruct((64, WIDE), BF16),
        ],
        cost_estimate=pl.CostEstimate(flops=4000000000, bytes_accessed=14000000, transcendentals=0),
        compiler_params=pltpu.CompilerParams(vmem_limit_bytes=POOL_VMEM),
        name="pool",
    )(keys, values)


def middle_kernel(own_ref, near_ref, far_ref, to_far_ref, l3_ref):
    to_far_ref[0:64, :] = far_ref[...]
    means = []
    for at in (BK, BV):
        rows = slice(at, at + 16)
        pair = own_ref[rows, :].astype(F32) + near_ref[rows, :].astype(F32)
        to_far_ref[rows, :] = pair.astype(BF16)
        means.append(jnp.sum(pair, axis=0, keepdims=True) * 0.0625)
    both = jnp.concatenate(means, axis=0).astype(BF16)
    l3_ref[...] = jnp.broadcast_to(both[None], l3_ref.shape)


def middle(own, near, far, copies):
    return pl.pallas_call(
        middle_kernel,
        out_shape=[
            jax.ShapeDtypeStruct((96, WIDE), BF16),
            jax.ShapeDtypeStruct((copies, 2, WIDE), BF16),
        ],
        cost_estimate=pl.CostEstimate(flops=1000000000, bytes_accessed=3500000, transcendentals=0),
        compiler_params=pltpu.CompilerParams(vmem_limit_bytes=4 * 1024 * 1024),
        name="middle",
    )(own, near, far)


def attend_kernel(
    total, base, info, q_ref, k_ref, kp_ref, kn_ref, v_ref, vp_ref, vn_ref, l1_ref, mid_ref, near_ref,
    far_ref, farther_ref, l3_ref, out_ref, kx, vx, l1x, sk, sv,
):
    step = pl.program_id(0)
    block = info[0]
    group = info[1 + base + step]
    odd = block % 2
    last_group = 2048 // 256 - 1

    @pl.when(step == 0)
    def _():
        for which, at in ((0, AK), (1, AV)):
            near, far = near_ref[at : at + 16, :], far_ref[at : at + 16, :]
            l1x[which, 0:16, :] = jnp.where(odd == 1, near, far)
            l1x[which, 16:144, :] = l1_ref[which]
            l1x[which, 144:160, :] = jnp.where(odd == 1, far, near)
        for scratch, at, which in ((sk, BK, 0), (sv, BV, 1)):
            scratch[48:64, :] = mid_ref[at : at + 16, :]
            scratch[64:80, :] = far_ref[at : at + 16, :]
            scratch[80:96, :] = farther_ref[at - BK : at - BK + 16, :]
            here = lax.broadcasted_iota(jnp.int32, (32, 2, WIDE), 1) == which
            picked = jnp.sum(jnp.where(here, l3_ref[...].astype(F32), 0.0), axis=1)
            scratch[96:128, :] = picked.astype(BF16)
        zeros = jnp.zeros((32, WIDE), BF16)
        kx[288:320, :] = zeros
        vx[288:320, :] = zeros

    for scratch, main, before, after, at in (
        (kx, k_ref, kp_ref, kn_ref, TK),
        (vx, v_ref, vp_ref, vn_ref, TV),
    ):
        near, far = near_ref[at : at + 16, :], far_ref[at : at + 16, :]
        low = jnp.where(odd == 1, near, far)
        high = jnp.where(odd == 1, far, near)
        scratch[0:16, :] = jnp.where(group == 0, low, before[...])
        scratch[16:272, :] = main[...]
        scratch[272:288, :] = jnp.where(group == last_group, high, after[...])
    window = pl.ds(pl.multiple_of(16 * group, 16), 48)
    sk[0:48, :] = l1x[0, window, :]
    sv[0:48, :] = l1x[1, window, :]

    c = 8 * block + group
    e = block // 2
    col = lax.broadcasted_iota(jnp.int32, (64, 128), 1)
    fine = lax.broadcasted_iota(jnp.int32, (64, 128), 0) // 16
    tile = col // 16
    beside = jnp.where(odd == 0, e - 1, e + 1)
    across = jnp.where(odd == 0, e + 1, e - 1)
    m = 16 * jnp.where(tile == 3, e, jnp.where(tile == 4, beside, across)) + col % 16
    term2 = jnp.where((m >= 0) & (m < total // 256) & (jnp.abs(m - c) > 1), 0.0, NEG)
    term3 = jnp.where(jnp.abs(col - 96 - e) > 1, 0.0, NEG)
    j = 16 * (c - 1) + col
    term1 = jnp.where((j >= 0) & (j < total // 16), 0.0, NEG)
    shared = jnp.where(col < 48, term1, jnp.where(col < 96, term2, term3))

    pairs = [(part, head) for part in range(4) for head in range(HEADS)]
    cols = [slice(HD * head, HD * head + HD) for head in range(HEADS)]
    rows = [slice(64 * part, 64 * part + 64) for part in range(4)]
    near_rows = [slice(64 * part, 64 * part + 128) for part in range(4)]
    biases = []
    for part in range(4):
        token = 256 * c + 64 * part - 16 + col
        ok = (jnp.abs(tile - 1 - fine) <= 1) & (token >= 0) & (token < total)
        own = (col < 48) & (jnp.abs(col - 16 - 4 * part - fine) <= 1)
        terms = [jnp.where(ok, 0.0, NEG), jnp.where(own, NEG, shared)]
        biases.append(jnp.concatenate(terms, axis=1).astype(F32))
    scores, weights, sums = [], [], []
    for part, head in pairs:
        key_rows = jnp.concatenate([kx[near_rows[part], cols[head]], sk[:, cols[head]]], axis=0)
        raw = lax.dot_general(
            q_ref[rows[part], cols[head]], key_rows, (((1,), (1,)), ((), ())), preferred_element_type=F32
        )
        scores.append(raw * SCORE + biases[part])
    peaks = [jnp.max(score, axis=1, keepdims=True) for score in scores]
    for score, peak in zip(scores, peaks):
        expo = jnp.exp2(score - peak)
        sums.append(jnp.sum(expo, axis=1, keepdims=True))
        weights.append(expo.astype(BF16))
    summed = []
    for (part, head), weight in zip(pairs, weights):
        value_rows = jnp.concatenate([vx[near_rows[part], cols[head]], sv[:, cols[head]]], axis=0)
        summed.append(jnp.dot(weight, value_rows, preferred_element_type=F32))
    for (part, head), value, sum_ in zip(pairs, summed, sums):
        out_ref[rows[part], cols[head]] = (value * (1.0 / sum_)).astype(BF16)


def attend(total, base, info, queries, keys, values, l1, mid, near, far, farther, l3):
    def main(i, s):
        return (s[1 + base + i], 0)

    def before(i, s):
        return (jnp.maximum(16 * s[1 + base + i] - 1, 0), 0)

    def after(i, s):
        return (jnp.minimum(16 * s[1 + base + i] + 16, 127), 0)

    def whole(array):
        return pl.BlockSpec(array.shape, lambda i, s: (0,) * array.ndim)

    wide, thin_low, thin_high = (
        pl.BlockSpec((256, WIDE), main),
        pl.BlockSpec((16, WIDE), before),
        pl.BlockSpec((16, WIDE), after),
    )
    small = (l1, mid, near, far, farther, l3)
    return pl.pallas_call(
        functools.partial(attend_kernel, total, base),
        grid_spec=pltpu.PrefetchScalarGridSpec(
            num_scalar_prefetch=1,
            grid=(2,),
            in_specs=[wide, wide, thin_low, thin_high, wide, thin_low, thin_high]
            + [whole(array) for array in small],
            out_specs=pl.BlockSpec((256, WIDE), lambda i, s: (i, 0)),
            scratch_shapes=[
                pltpu.VMEM((320, WIDE), BF16),
                pltpu.VMEM((320, WIDE), BF16),
                pltpu.VMEM((2, 160, WIDE), BF16),
                pltpu.VMEM((128, WIDE), BF16),
                pltpu.VMEM((128, WIDE), BF16),
            ],
        ),
        out_shape=jax.ShapeDtypeStruct((512, WIDE), BF16),
        cost_estimate=pl.CostEstimate(flops=20000000000, bytes_accessed=70000000, transcendentals=0),
        compiler_params=pltpu.CompilerParams(vmem_limit_bytes=ATTEND_VMEM),
        name="attend",
    )(info, queries, keys, keys, keys, values, values, values, *small)


def project_kernel(n, m, *refs):
    weights, attended, before, out_ref = refs[:m], refs[m : n + m], refs[n + m : -1], refs[-1]
    left = jnp.concatenate([a[...] for a in attended], axis=1)
    right = jnp.concatenate([w[...] for w in weights], axis=0)
    total = jnp.dot(left, right, preferred_element_type=F32)
    if before:
        total += before[0][...]
    out_ref[...] = total.astype(out_ref.dtype)


def project(attended, weights, before, dtype):
    rows, columns = attended[0].shape[0], weights[0].shape[1]
    tile = 1024
    depth = WIDE * len(attended)

    def tiles(arrays):
        return [pl.BlockSpec((w.shape[0], tile), lambda i: (0, i)) for w in arrays]

    return pl.pallas_call(
        functools.partial(project_kernel, len(attended), len(weights)),
        grid=(columns // tile,),
        in_specs=[
            *tiles(weights),
            *(pl.BlockSpec(a.shape, lambda i: (0, 0)) for a in attended),
            *tiles(before),
        ],
        out_specs=pl.BlockSpec((rows, tile), lambda i: (0, i)),
        out_shape=jax.ShapeDtypeStruct((rows, columns), dtype),
        cost_estimate=pl.CostEstimate(flops=20000000000, bytes_accessed=70000000, transcendentals=0),
        compiler_params=pltpu.CompilerParams(vmem_limit_bytes=PROJECT_VMEM),
        name="project",
    )(*weights, *attended, *before)


def body(queries, keys, values, out_weight):
    blocks = lax.axis_size("seq")
    total = queries.shape[0] * blocks
    s = lax.axis_index("seq")
    h = lax.axis_index("head")

    def permute(array, move):
        return lax.ppermute(array, "seq", [(i, move(i) % blocks) for i in range(blocks)])

    def swap(array, bit):
        return lax.ppermute(array, "head", [(i, i ^ bit) for i in range(4)])

    def cross(array):
        pairs = []
        for i in range(blocks):
            for j in range(4):
                pairs.append((4 * i + j, 4 * (i ^ 8 if j % 2 else i) + (j ^ 2)))
        return lax.ppermute(array, ("seq", "head"), pairs)

    order = (2, 1, 3, 0)
    groups = [2 * (h ^ bit) + part for bit in order for part in range(2)]
    info = jnp.stack([s, *groups]).astype(jnp.int32)

    w_far = cross(out_weight)
    w_near = swap(out_weight, 1)
    l1, to_near, to_far = pool(keys, values)
    near = permute(to_near, lambda i: i ^ 1)
    to_far, l3 = middle(to_near, near, to_far, blocks // 2)
    far = permute(to_far, lambda i: i + 1 if i % 2 else i - 1)
    farther = permute(far[BK:, :], lambda i: i ^ 1)
    peers = [[2 * i + parity for i in range(blocks // 2)] for parity in range(2)]
    l3 = lax.all_to_all(l3, "seq", 0, 0, axis_index_groups=peers)

    w_far, far = lax.optimization_barrier((w_far, far))
    w_cross = swap(w_far, 1)
    outs = {}
    for at, bit in ORDER:
        part = attend(total, 2 * at, info, queries, keys, values, l1, to_far, near, far, farther, l3)
        outs[bit] = swap(part, bit) if bit else part

    inner = project([outs[0], outs[2], outs[1]], [out_weight, w_far, w_near], [], F32)
    return project([outs[3]], [w_cross], [inner], BF16)


def solution(mesh):
    placed = (P("seq", "head"), P("seq", "head"), P("seq", "head"), P("head", None))
    return jax.shard_map(
        body, mesh=mesh, in_specs=placed, out_specs=P(("seq", "head"), None), check_vma=False
    )
```

```python
import functools

import jax
import jax.numpy as jnp
from jax import lax
from jax.experimental import pallas as pl
from jax.experimental.pallas import tpu as pltpu
from jax.sharding import PartitionSpec as P

HD = 128
HEADS = 4
WIDE = HEADS * HD
LOG2E = 1.4426950408889634
SCORE = HD**-0.5 * LOG2E
NEG = -1e30
F32 = jnp.float32
BF16 = jnp.bfloat16
POOL_VMEM, ATTEND_VMEM, PROJECT_VMEM = (mib * 1024 * 1024 for mib in (53, 51, 24))
CHUNKS = 4
ATTEND_COST = pl.CostEstimate(flops=20000000000, bytes_accessed=70000000, transcendentals=0)
SMALL = pl.CostEstimate(flops=1000, bytes_accessed=1000, transcendentals=0)

TK, TV, AK, AV, BK, BV = (16 * i for i in range(6))


def mean_rows(count, size, scale):
    rows = lax.broadcasted_iota(jnp.int32, (count, count * size), 0)
    cols = lax.broadcasted_iota(jnp.int32, (count, count * size), 1)
    return jnp.where(rows == cols // size, scale, 0.0).astype(BF16)


def pool_kernel(k_hbm, v_hbm, l1_ref, near_ref, far_ref, k_ref, v_ref, sems):
    odd = lax.axis_index("seq") % 2
    ones = mean_rows(16, 16, 1.0)
    chunk = k_ref.shape[0] // CHUNKS
    copies = []
    for i in range(CHUNKS):
        rows = pl.ds(chunk * i, chunk)
        for which, (hbm, ref) in enumerate(((k_hbm, k_ref), (v_hbm, v_ref))):
            copy = pltpu.make_async_copy(hbm.at[rows, :], ref.at[rows, :], sems.at[which, i])
            copy.start()
            copies.append(copy)
    level2 = [[], []]
    for i in range(CHUNKS):
        for which, ref in enumerate((k_ref, v_ref)):
            copies[2 * i + which].wait()
            for at in range(chunk * i, chunk * (i + 1), 256):
                total = jnp.dot(ones, ref[at : at + 256, :], preferred_element_type=F32)
                l1_ref[which, at // 16 : at // 16 + 16, :] = (total * 0.0625).astype(BF16)
                level2[which].append(jnp.sum(total, axis=0, keepdims=True) * (1.0 / 256.0))

    last = k_ref.shape[0]
    low = [k_ref[0:16, :], v_ref[0:16, :], l1_ref[0, 0:16, :], l1_ref[1, 0:16, :]]
    high = [k_ref[last - 16 : last, :], v_ref[last - 16 : last, :]]
    high += [l1_ref[which, last // 16 - 16 : last // 16, :] for which in range(2)]
    for at, (below, above) in enumerate(zip(low, high)):
        rows = slice(16 * at, 16 * at + 16)
        near_ref[rows, :] = jnp.where(odd == 1, below, above)
        far_ref[rows, :] = jnp.where(odd == 1, above, below)
    row = lax.broadcasted_iota(jnp.int32, (16, WIDE), 0)
    for which, at in ((0, BK), (1, BV)):
        both = jnp.concatenate(level2[which] * 2, axis=0)
        near_ref[at : at + 16, :] = jnp.where(row // 8 == odd, both, 0.0).astype(BF16)


def pool(keys, values):
    rows = keys.shape[0]
    return pl.pallas_call(
        pool_kernel,
        in_specs=[
            pl.BlockSpec(memory_space=pltpu.HBM),
            pl.BlockSpec(memory_space=pltpu.HBM),
        ],
        out_specs=[pl.BlockSpec(memory_space=pltpu.VMEM)] * 3,
        scratch_shapes=[
            pltpu.VMEM((rows, WIDE), BF16),
            pltpu.VMEM((rows, WIDE), BF16),
            pltpu.SemaphoreType.DMA((2, CHUNKS)),
        ],
        out_shape=[
            jax.ShapeDtypeStruct((2, rows // 16, WIDE), BF16),
            jax.ShapeDtypeStruct((96, WIDE), BF16),
            jax.ShapeDtypeStruct((64, WIDE), BF16),
        ],
        cost_estimate=pl.CostEstimate(flops=4000000000, bytes_accessed=14000000, transcendentals=0),
        compiler_params=pltpu.CompilerParams(vmem_limit_bytes=POOL_VMEM),
        name="pool",
    )(keys, values)


def middle_kernel(own_ref, near_ref, far_ref, to_far_ref, l3_ref):
    to_far_ref[0:64, :] = far_ref[...]
    means = []
    for at in (BK, BV):
        rows = slice(at, at + 16)
        pair = own_ref[rows, :].astype(F32) + near_ref[rows, :].astype(F32)
        to_far_ref[rows, :] = pair.astype(BF16)
        mean = jnp.sum(pair, axis=0, keepdims=True) * 0.0625
        means += [mean[:, HD * head : HD * head + HD] for head in range(HEADS)]
    both = jnp.concatenate(means, axis=0).astype(BF16)
    l3_ref[...] = jnp.broadcast_to(both[None], l3_ref.shape)


def middle(own, near, far, copies):
    return pl.pallas_call(
        middle_kernel,
        out_shape=[
            jax.ShapeDtypeStruct((96, WIDE), BF16),
            jax.ShapeDtypeStruct((copies, 2 * HEADS, HD), BF16),
        ],
        cost_estimate=pl.CostEstimate(flops=1000000000, bytes_accessed=3500000, transcendentals=0),
        compiler_params=pltpu.CompilerParams(vmem_limit_bytes=4 * 1024 * 1024),
        name="middle",
    )(own, near, far)


def attend_kernel(
    total, base, info, q_ref, k_ref, kp_ref, kn_ref, v_ref, vp_ref, vn_ref, l1_ref, mid_ref, near_ref,
    far_ref, farther_ref, l3_ref, out_ref, kx, vx, l1x, sk, sv,
):
    step = pl.program_id(0)
    block = info[0]
    group = info[1 + base + step]
    odd = block % 2
    last_group = 2048 // 256 - 1

    @pl.when(step == 0)
    def _():
        for which, at in ((0, AK), (1, AV)):
            near, far = near_ref[at : at + 16, :], far_ref[at : at + 16, :]
            l1x[which, 0:16, :] = jnp.where(odd == 1, near, far)
            l1x[which, 16:144, :] = l1_ref[which]
            l1x[which, 144:160, :] = jnp.where(odd == 1, far, near)
        parts = 2 * HEADS * l3_ref.shape[0]
        wanted = lax.broadcasted_iota(jnp.int32, (parts, parts), 0)
        given = lax.broadcasted_iota(jnp.int32, (parts, parts), 1)
        pick = given == 2 * HEADS * (wanted % 32) + wanted // 32
        level3 = jnp.dot(
            jnp.where(pick, 1.0, 0.0).astype(BF16),
            l3_ref[...].reshape(parts, HD),
            preferred_element_type=F32,
        ).astype(BF16)
        for scratch, at, which in ((sk, BK, 0), (sv, BV, 1)):
            scratch[48:64, :] = mid_ref[at : at + 16, :]
            scratch[64:80, :] = far_ref[at : at + 16, :]
            scratch[80:96, :] = farther_ref[at - BK : at - BK + 16, :]
            for head in range(HEADS):
                first = 32 * (HEADS * which + head)
                scratch[96:128, HD * head : HD * head + HD] = level3[first : first + 32, :]
        zeros = jnp.zeros((32, WIDE), BF16)
        kx[288:320, :] = zeros
        vx[288:320, :] = zeros

    for scratch, main, before, after, at in (
        (kx, k_ref, kp_ref, kn_ref, TK),
        (vx, v_ref, vp_ref, vn_ref, TV),
    ):
        near, far = near_ref[at : at + 16, :], far_ref[at : at + 16, :]
        low = jnp.where(odd == 1, near, far)
        high = jnp.where(odd == 1, far, near)
        scratch[0:16, :] = jnp.where(group == 0, low, before[...])
        scratch[16:272, :] = main[...]
        scratch[272:288, :] = jnp.where(group == last_group, high, after[...])
    window = pl.ds(pl.multiple_of(16 * group, 16), 48)
    sk[0:48, :] = l1x[0, window, :]
    sv[0:48, :] = l1x[1, window, :]

    c = 8 * block + group
    e = block // 2
    col = lax.broadcasted_iota(jnp.int32, (64, 128), 1)
    fine = lax.broadcasted_iota(jnp.int32, (64, 128), 0) // 16
    tile = col // 16
    beside = jnp.where(odd == 0, e - 1, e + 1)
    across = jnp.where(odd == 0, e + 1, e - 1)
    m = 16 * jnp.where(tile == 3, e, jnp.where(tile == 4, beside, across)) + col % 16
    term2 = jnp.where((m >= 0) & (m < total // 256) & (jnp.abs(m - c) > 1), 0.0, NEG)
    term3 = jnp.where(jnp.abs(col - 96 - e) > 1, 0.0, NEG)
    j = 16 * (c - 1) + col
    term1 = jnp.where((j >= 0) & (j < total // 16), 0.0, NEG)
    shared = jnp.where(col < 48, term1, jnp.where(col < 96, term2, term3))

    pairs = [(part, head) for part in range(4) for head in range(HEADS)]
    cols = [slice(HD * head, HD * head + HD) for head in range(HEADS)]
    rows = [slice(64 * part, 64 * part + 64) for part in range(4)]
    near_rows = [slice(64 * part, 64 * part + 128) for part in range(4)]
    biases = []
    for part in range(4):
        token = 256 * c + 64 * part - 16 + col
        ok = (jnp.abs(tile - 1 - fine) <= 1) & (token >= 0) & (token < total)
        own = (col < 48) & (jnp.abs(col - 16 - 4 * part - fine) <= 1)
        terms = [jnp.where(ok, 0.0, NEG), jnp.where(own, NEG, shared)]
        biases.append(jnp.concatenate(terms, axis=1).astype(F32))
    scores, weights, sums = [], [], []
    for part, head in pairs:
        key_rows = jnp.concatenate([kx[near_rows[part], cols[head]], sk[:, cols[head]]], axis=0)
        raw = lax.dot_general(
            q_ref[rows[part], cols[head]], key_rows, (((1,), (1,)), ((), ())), preferred_element_type=F32
        )
        scores.append(raw * SCORE + biases[part])
    peaks = [jnp.max(score, axis=1, keepdims=True) for score in scores]
    for score, peak in zip(scores, peaks):
        expo = jnp.exp2(score - peak)
        sums.append(jnp.sum(expo, axis=1, keepdims=True))
        weights.append(expo.astype(BF16))
    summed = []
    for (part, head), weight in zip(pairs, weights):
        value_rows = jnp.concatenate([vx[near_rows[part], cols[head]], sv[:, cols[head]]], axis=0)
        summed.append(jnp.dot(weight, value_rows, preferred_element_type=F32))
    for (part, head), value, sum_ in zip(pairs, summed, sums):
        out_ref[rows[part], cols[head]] = (value * (1.0 / sum_)).astype(BF16)


def windows(base):
    def main(i, s):
        return (s[1 + base + i], 0)

    def before(i, s):
        return (jnp.maximum(16 * s[1 + base + i] - 1, 0), 0)

    def after(i, s):
        return (jnp.minimum(16 * s[1 + base + i] + 16, 127), 0)

    wide, thin_low, thin_high = (
        pl.BlockSpec((256, WIDE), main),
        pl.BlockSpec((16, WIDE), before),
        pl.BlockSpec((16, WIDE), after),
    )
    return [wide, wide, thin_low, thin_high, wide, thin_low, thin_high]


def attend(total, base, steps, info, rows, small):
    def whole(array):
        return pl.BlockSpec(array.shape, lambda i, s: (0,) * array.ndim)

    return pl.pallas_call(
        functools.partial(attend_kernel, total, base),
        grid_spec=pltpu.PrefetchScalarGridSpec(
            num_scalar_prefetch=1,
            grid=(steps,),
            in_specs=windows(base) + [whole(array) for array in small],
            out_specs=pl.BlockSpec((256, WIDE), lambda i, s: (i, 0)),
            scratch_shapes=[
                pltpu.VMEM((320, WIDE), BF16),
                pltpu.VMEM((320, WIDE), BF16),
                pltpu.VMEM((2, 160, WIDE), BF16),
                pltpu.VMEM((128, WIDE), BF16),
                pltpu.VMEM((128, WIDE), BF16),
            ],
        ),
        out_shape=jax.ShapeDtypeStruct((256 * steps, WIDE), BF16),
        cost_estimate=ATTEND_COST,
        compiler_params=pltpu.CompilerParams(vmem_limit_bytes=ATTEND_VMEM),
        name="attend",
    )(info, *rows, *small)


def project_kernel(ahead, n, m, *refs):
    refs = refs[ahead:]
    before, weights, attended, out_ref = refs[: -n - m - 1], refs[-n - m - 1 : -n - 1], refs[-n - 1 : -1], refs[-1]
    whole, halves = [], []
    for a in attended:
        if a.shape[0] == out_ref.shape[0]:
            whole.append(a[...])
        else:
            halves.append(a[...])
            if len(halves) == 2:
                whole.append(jnp.concatenate(halves, axis=0))
                halves = []
    left = jnp.concatenate(whole, axis=1)
    right = jnp.concatenate([w[...] for w in weights], axis=0)
    total = jnp.dot(left, right, preferred_element_type=F32)
    if before:
        total += before[0][...]
    out_ref[...] = total.astype(out_ref.dtype)


def project(attended, weights, before, dtype, ahead=()):
    rows, columns = attended[0].shape[0], weights[0].shape[1]
    tile = 1024
    depth = sum(w.shape[0] for w in weights)

    def tiles(arrays):
        return [pl.BlockSpec((w.shape[0], tile), lambda i: (0, i)) for w in arrays]

    return pl.pallas_call(
        functools.partial(project_kernel, len(ahead), len(attended), len(weights)),
        grid=(columns // tile,),
        in_specs=[
            *(pl.BlockSpec(memory_space=pl.ANY) for _ in ahead),
            *tiles(before),
            *tiles(weights),
            *(pl.BlockSpec(a.shape, lambda i: (0, 0)) for a in attended),
        ],
        out_specs=pl.BlockSpec((rows, tile), lambda i: (0, i)),
        out_shape=jax.ShapeDtypeStruct((rows, columns), dtype),
        cost_estimate=pl.CostEstimate(flops=20000000000, bytes_accessed=70000000, transcendentals=0),
        compiler_params=pltpu.CompilerParams(vmem_limit_bytes=PROJECT_VMEM),
        name="project",
    )(*ahead, *before, *weights, *attended)


def body(queries, keys, values, out_weight):
    blocks = lax.axis_size("seq")
    total = queries.shape[0] * blocks
    s = lax.axis_index("seq")
    h = lax.axis_index("head")

    def permute(array, move):
        return lax.ppermute(array, "seq", [(i, move(i) % blocks) for i in range(blocks)])

    def swap(array, bit):
        return lax.ppermute(array, "head", [(i, i ^ bit) for i in range(4)])

    def cross(array):
        pairs = []
        for i in range(blocks):
            for j in range(4):
                pairs.append((4 * i + j, 4 * (i ^ 8 if j % 2 else i) + (j ^ 2)))
        return lax.ppermute(array, ("seq", "head"), pairs)

    order = (2, 3, 1, 0)
    groups = [2 * (h ^ bit) + part for bit in order for part in range(2)]
    info = jnp.stack([s, *groups]).astype(jnp.int32)

    w_far = cross(out_weight)
    w_near = swap(out_weight, 1)
    l1, to_near, to_far = pool(keys, values)
    near = permute(to_near, lambda i: i ^ 1)
    to_far, l3 = middle(to_near, near, to_far, blocks // 2)
    far = permute(to_far, lambda i: i + 1 if i % 2 else i - 1)
    farther = permute(to_far[BK:, :], lambda i: i + 2 if i % 2 else i - 2)
    peers = [[2 * i + parity for i in range(blocks // 2)] for parity in range(2)]
    l3 = lax.all_to_all(l3, "seq", 0, 0, axis_index_groups=peers)

    w_far, w_near, far = lax.optimization_barrier((w_far, w_near, far))
    w_cross = swap(w_far, 1)
    rows = (queries, keys, keys, keys, values, values, values)
    small = (l1, to_far, near, far, farther, l3)
    foreign = [swap(attend(total, part, 1, info, rows, small), 2) for part in range(2)]
    last = swap(attend(total, 2, 2, info, rows, small), 3)
    inside = swap(attend(total, 4, 2, info, rows, small), 1)
    own = attend(total, 6, 2, info, rows, small)

    inner = project([own, *foreign, inside], [out_weight, w_far, w_near], [], F32)
    return project([last], [w_cross], [inner], BF16, [*foreign, last])


def solution(mesh):
    placed = (P("seq", "head"), P("seq", "head"), P("seq", "head"), P("head", None))
    return jax.shard_map(
        body, mesh=mesh, in_specs=placed, out_specs=P(("seq", "head"), None), check_vma=False
    )
```

```python
import functools

import jax
import jax.numpy as jnp
from jax import lax
from jax.experimental import pallas as pl
from jax.experimental.pallas import tpu as pltpu
from jax.sharding import PartitionSpec as P

HD = 128
HEADS = 4
WIDE = HEADS * HD
LOG2E = 1.4426950408889634
SCORE = HD**-0.5 * LOG2E
NEG = -1e30
F32 = jnp.float32
BF16 = jnp.bfloat16
POOL_VMEM, ATTEND_VMEM, PROJECT_VMEM = (mib * 1024 * 1024 for mib in (53, 51, 24))
CHUNKS = 4
PROJECT_COST = pl.CostEstimate(flops=20000000000, bytes_accessed=70000000, transcendentals=0)
ATTEND_COST = pl.CostEstimate(flops=20000000000, bytes_accessed=70000000, transcendentals=0)
SMALL = pl.CostEstimate(flops=1000, bytes_accessed=1000, transcendentals=0)

TK, TV, AK, AV, BK, BV = (16 * i for i in range(6))


def mean_rows(count, size, scale):
    rows = lax.broadcasted_iota(jnp.int32, (count, count * size), 0)
    cols = lax.broadcasted_iota(jnp.int32, (count, count * size), 1)
    return jnp.where(rows == cols // size, scale, 0.0).astype(BF16)


def pool_kernel(k_hbm, v_hbm, l1_ref, near_ref, far_ref, k_ref, v_ref, sems):
    odd = lax.axis_index("seq") % 2
    ones = mean_rows(16, 16, 1.0)
    chunk = k_ref.shape[0] // CHUNKS
    copies = []
    for i in range(CHUNKS):
        rows = pl.ds(chunk * i, chunk)
        for which, (hbm, ref) in enumerate(((k_hbm, k_ref), (v_hbm, v_ref))):
            copy = pltpu.make_async_copy(hbm.at[rows, :], ref.at[rows, :], sems.at[which, i])
            copy.start()
            copies.append(copy)
    level2 = [[], []]
    for i in range(CHUNKS):
        for which, ref in enumerate((k_ref, v_ref)):
            copies[2 * i + which].wait()
            for at in range(chunk * i, chunk * (i + 1), 256):
                total = jnp.dot(ones, ref[at : at + 256, :], preferred_element_type=F32)
                l1_ref[which, at // 16 : at // 16 + 16, :] = (total * 0.0625).astype(BF16)
                level2[which].append(jnp.sum(total, axis=0, keepdims=True) * (1.0 / 256.0))

    last = k_ref.shape[0]
    low = [k_ref[0:16, :], v_ref[0:16, :], l1_ref[0, 0:16, :], l1_ref[1, 0:16, :]]
    high = [k_ref[last - 16 : last, :], v_ref[last - 16 : last, :]]
    high += [l1_ref[which, last // 16 - 16 : last // 16, :] for which in range(2)]
    for at, (below, above) in enumerate(zip(low, high)):
        rows = slice(16 * at, 16 * at + 16)
        near_ref[rows, :] = jnp.where(odd == 1, below, above)
        far_ref[rows, :] = jnp.where(odd == 1, above, below)
    row = lax.broadcasted_iota(jnp.int32, (16, WIDE), 0)
    for which, at in ((0, BK), (1, BV)):
        both = jnp.concatenate(level2[which] * 2, axis=0)
        near_ref[at : at + 16, :] = jnp.where(row // 8 == odd, both, 0.0).astype(BF16)


def pool(keys, values):
    rows = keys.shape[0]
    return pl.pallas_call(
        pool_kernel,
        in_specs=[
            pl.BlockSpec(memory_space=pltpu.HBM),
            pl.BlockSpec(memory_space=pltpu.HBM),
        ],
        out_specs=[pl.BlockSpec(memory_space=pltpu.VMEM)] * 3,
        scratch_shapes=[
            pltpu.VMEM((rows, WIDE), BF16),
            pltpu.VMEM((rows, WIDE), BF16),
            pltpu.SemaphoreType.DMA((2, CHUNKS)),
        ],
        out_shape=[
            jax.ShapeDtypeStruct((2, rows // 16, WIDE), BF16),
            jax.ShapeDtypeStruct((96, WIDE), BF16),
            jax.ShapeDtypeStruct((64, WIDE), BF16),
        ],
        cost_estimate=pl.CostEstimate(flops=4000000000, bytes_accessed=14000000, transcendentals=0),
        compiler_params=pltpu.CompilerParams(vmem_limit_bytes=POOL_VMEM),
        name="pool",
    )(keys, values)


def middle_kernel(own_ref, near_ref, far_ref, to_far_ref, l3_ref):
    to_far_ref[0:64, :] = far_ref[...]
    means = []
    for at in (BK, BV):
        rows = slice(at, at + 16)
        pair = own_ref[rows, :].astype(F32) + near_ref[rows, :].astype(F32)
        to_far_ref[rows, :] = pair.astype(BF16)
        mean = jnp.sum(pair, axis=0, keepdims=True) * 0.0625
        means += [mean[:, HD * head : HD * head + HD] for head in range(HEADS)]
    both = jnp.concatenate(means, axis=0).astype(BF16)
    l3_ref[...] = jnp.broadcast_to(both[None], l3_ref.shape)


def middle(own, near, far, copies):
    return pl.pallas_call(
        middle_kernel,
        out_shape=[
            jax.ShapeDtypeStruct((96, WIDE), BF16),
            jax.ShapeDtypeStruct((copies, 2 * HEADS, HD), BF16),
        ],
        cost_estimate=pl.CostEstimate(flops=1000000000, bytes_accessed=3500000, transcendentals=0),
        compiler_params=pltpu.CompilerParams(vmem_limit_bytes=4 * 1024 * 1024),
        name="middle",
    )(own, near, far)


def attend_kernel(
    total, base, info, q_ref, k_ref, kp_ref, kn_ref, v_ref, vp_ref, vn_ref, l1_ref, mid_ref, near_ref,
    far_ref, farther_ref, l3_ref, out_ref, kx, vx, l1x, sk, sv,
):
    step = pl.program_id(0)
    block = info[0]
    group = info[1 + base + step]
    odd = block % 2
    last_group = 2048 // 256 - 1

    @pl.when(step == 0)
    def _():
        for which, at in ((0, AK), (1, AV)):
            near, far = near_ref[at : at + 16, :], far_ref[at : at + 16, :]
            l1x[which, 0:16, :] = jnp.where(odd == 1, near, far)
            l1x[which, 16:144, :] = l1_ref[which]
            l1x[which, 144:160, :] = jnp.where(odd == 1, far, near)
        parts = 2 * HEADS * l3_ref.shape[0]
        wanted = lax.broadcasted_iota(jnp.int32, (parts, parts), 0)
        given = lax.broadcasted_iota(jnp.int32, (parts, parts), 1)
        pick = given == 2 * HEADS * (wanted % 32) + wanted // 32
        level3 = jnp.dot(
            jnp.where(pick, 1.0, 0.0).astype(BF16),
            l3_ref[...].reshape(parts, HD),
            preferred_element_type=F32,
        ).astype(BF16)
        for scratch, at, which in ((sk, BK, 0), (sv, BV, 1)):
            scratch[48:64, :] = mid_ref[at : at + 16, :]
            scratch[64:80, :] = far_ref[at : at + 16, :]
            scratch[80:96, :] = farther_ref[at - BK : at - BK + 16, :]
            for head in range(HEADS):
                first = 32 * (HEADS * which + head)
                scratch[96:128, HD * head : HD * head + HD] = level3[first : first + 32, :]
        zeros = jnp.zeros((32, WIDE), BF16)
        kx[288:320, :] = zeros
        vx[288:320, :] = zeros

    for scratch, main, before, after, at in (
        (kx, k_ref, kp_ref, kn_ref, TK),
        (vx, v_ref, vp_ref, vn_ref, TV),
    ):
        near, far = near_ref[at : at + 16, :], far_ref[at : at + 16, :]
        low = jnp.where(odd == 1, near, far)
        high = jnp.where(odd == 1, far, near)
        scratch[0:16, :] = jnp.where(group == 0, low, before[...])
        scratch[16:272, :] = main[...]
        scratch[272:288, :] = jnp.where(group == last_group, high, after[...])
    window = pl.ds(pl.multiple_of(16 * group, 16), 48)
    sk[0:48, :] = l1x[0, window, :]
    sv[0:48, :] = l1x[1, window, :]

    c = 8 * block + group
    e = block // 2
    col = lax.broadcasted_iota(jnp.int32, (64, 128), 1)
    fine = lax.broadcasted_iota(jnp.int32, (64, 128), 0) // 16
    tile = col // 16
    beside = jnp.where(odd == 0, e - 1, e + 1)
    across = jnp.where(odd == 0, e + 1, e - 1)
    m = 16 * jnp.where(tile == 3, e, jnp.where(tile == 4, beside, across)) + col % 16
    term2 = jnp.where((m >= 0) & (m < total // 256) & (jnp.abs(m - c) > 1), 0.0, NEG)
    term3 = jnp.where(jnp.abs(col - 96 - e) > 1, 0.0, NEG)
    j = 16 * (c - 1) + col
    term1 = jnp.where((j >= 0) & (j < total // 16), 0.0, NEG)
    shared = jnp.where(col < 48, term1, jnp.where(col < 96, term2, term3))

    pairs = [(part, head) for part in range(4) for head in range(HEADS)]
    cols = [slice(HD * head, HD * head + HD) for head in range(HEADS)]
    rows = [slice(64 * part, 64 * part + 64) for part in range(4)]
    near_rows = [slice(64 * part, 64 * part + 128) for part in range(4)]
    biases = []
    for part in range(4):
        token = 256 * c + 64 * part - 16 + col
        ok = (jnp.abs(tile - 1 - fine) <= 1) & (token >= 0) & (token < total)
        own = (col < 48) & (jnp.abs(col - 16 - 4 * part - fine) <= 1)
        terms = [jnp.where(ok, 0.0, NEG), jnp.where(own, NEG, shared)]
        biases.append(jnp.concatenate(terms, axis=1).astype(F32))
    scores, weights, sums = [], [], []
    for part, head in pairs:
        key_rows = jnp.concatenate([kx[near_rows[part], cols[head]], sk[:, cols[head]]], axis=0)
        raw = lax.dot_general(
            q_ref[rows[part], cols[head]], key_rows, (((1,), (1,)), ((), ())), preferred_element_type=F32
        )
        scores.append(raw * SCORE + biases[part])
    peaks = [jnp.max(score, axis=1, keepdims=True) for score in scores]
    for score, peak in zip(scores, peaks):
        expo = jnp.exp2(score - peak)
        sums.append(jnp.sum(expo, axis=1, keepdims=True))
        weights.append(expo.astype(BF16))
    summed = []
    for (part, head), weight in zip(pairs, weights):
        value_rows = jnp.concatenate([vx[near_rows[part], cols[head]], sv[:, cols[head]]], axis=0)
        summed.append(jnp.dot(weight, value_rows, preferred_element_type=F32))
    for (part, head), value, sum_ in zip(pairs, summed, sums):
        out_ref[rows[part], cols[head]] = (value * (1.0 / sum_)).astype(BF16)


def windows(base):
    def main(i, s):
        return (s[1 + base + i], 0)

    def before(i, s):
        return (jnp.maximum(16 * s[1 + base + i] - 1, 0), 0)

    def after(i, s):
        return (jnp.minimum(16 * s[1 + base + i] + 16, 127), 0)

    wide, thin_low, thin_high = (
        pl.BlockSpec((256, WIDE), main),
        pl.BlockSpec((16, WIDE), before),
        pl.BlockSpec((16, WIDE), after),
    )
    return [wide, wide, thin_low, thin_high, wide, thin_low, thin_high]


def attend(total, base, steps, info, rows, small):
    def whole(array):
        return pl.BlockSpec(array.shape, lambda i, s: (0,) * array.ndim)

    return pl.pallas_call(
        functools.partial(attend_kernel, total, base),
        grid_spec=pltpu.PrefetchScalarGridSpec(
            num_scalar_prefetch=1,
            grid=(steps,),
            in_specs=windows(base) + [whole(array) for array in small],
            out_specs=pl.BlockSpec((256, WIDE), lambda i, s: (i, 0)),
            scratch_shapes=[
                pltpu.VMEM((320, WIDE), BF16),
                pltpu.VMEM((320, WIDE), BF16),
                pltpu.VMEM((2, 160, WIDE), BF16),
                pltpu.VMEM((128, WIDE), BF16),
                pltpu.VMEM((128, WIDE), BF16),
            ],
        ),
        out_shape=jax.ShapeDtypeStruct((256 * steps, WIDE), BF16),
        cost_estimate=ATTEND_COST,
        compiler_params=pltpu.CompilerParams(vmem_limit_bytes=ATTEND_VMEM),
        name="attend",
    )(info, *rows, *small)


def project_kernel(ahead, n, m, *refs):
    refs = refs[ahead:]
    before, weights, attended, out_ref = refs[: -n - m - 1], refs[-n - m - 1 : -n - 1], refs[-n - 1 : -1], refs[-1]
    whole, halves = [], []
    for a in attended:
        if a.shape[0] == out_ref.shape[0]:
            whole.append(a[...])
        else:
            halves.append(a[...])
            if len(halves) == 2:
                whole.append(jnp.concatenate(halves, axis=0))
                halves = []
    left = jnp.concatenate(whole, axis=1)
    right = jnp.concatenate([w[...] for w in weights], axis=0)
    total = jnp.dot(left, right, preferred_element_type=F32)
    if before:
        total += before[0][...]
    out_ref[...] = total.astype(out_ref.dtype)


def project(attended, weights, before, dtype, ahead=()):
    rows, columns = attended[0].shape[0], weights[0].shape[1]
    tile = 1024
    depth = sum(w.shape[0] for w in weights)

    def tiles(arrays):
        return [pl.BlockSpec((w.shape[0], tile), lambda i: (0, i)) for w in arrays]

    return pl.pallas_call(
        functools.partial(project_kernel, len(ahead), len(attended), len(weights)),
        grid=(columns // tile,),
        in_specs=[
            *(pl.BlockSpec(memory_space=pl.ANY) for _ in ahead),
            *tiles(before),
            *tiles(weights),
            *(pl.BlockSpec(a.shape, lambda i: (0, 0)) for a in attended),
        ],
        out_specs=pl.BlockSpec((rows, tile), lambda i: (0, i)),
        out_shape=jax.ShapeDtypeStruct((rows, columns), dtype),
        cost_estimate=pl.CostEstimate(flops=20000000000, bytes_accessed=70000000, transcendentals=0),
        compiler_params=pltpu.CompilerParams(vmem_limit_bytes=PROJECT_VMEM),
        name="project",
    )(*ahead, *before, *weights, *attended)


def finish_kernel(ahead, *refs):
    before, weight, attended, out, tiles, sems = refs[ahead:]
    width = tiles.shape[2]
    copies = []
    for i in range(tiles.shape[0]):
        cols = slice(width * i, width * i + width)
        total = jnp.dot(attended[...], weight[:, cols], preferred_element_type=F32) + before[:, cols]
        tiles[i] = total.astype(BF16)
        copies.append(pltpu.make_async_copy(tiles.at[i], out.at[:, pl.ds(width * i, width)], sems.at[i]))
        copies[-1].start()
    for copy in copies:
        copy.wait()


def finish(attended, weight, before, ahead):
    rows, columns = before.shape
    tiles = 4
    return pl.pallas_call(
        functools.partial(finish_kernel, len(ahead)),
        in_specs=[pl.BlockSpec(memory_space=pl.ANY) for _ in ahead]
        + [pl.BlockSpec(memory_space=pltpu.VMEM)] * 3,
        out_specs=pl.BlockSpec(memory_space=pl.ANY),
        scratch_shapes=[
            pltpu.VMEM((tiles, rows, columns // tiles), BF16),
            pltpu.SemaphoreType.DMA((tiles,)),
        ],
        out_shape=jax.ShapeDtypeStruct((rows, columns), BF16),
        cost_estimate=PROJECT_COST,
        compiler_params=pltpu.CompilerParams(vmem_limit_bytes=PROJECT_VMEM),
        name="finish",
    )(*ahead, before, weight, attended)


def body(queries, keys, values, out_weight):
    blocks = lax.axis_size("seq")
    total = queries.shape[0] * blocks
    s = lax.axis_index("seq")
    h = lax.axis_index("head")

    def permute(array, move):
        return lax.ppermute(array, "seq", [(i, move(i) % blocks) for i in range(blocks)])

    def swap(array, bit):
        return lax.ppermute(array, "head", [(i, i ^ bit) for i in range(4)])

    def cross(array):
        pairs = []
        for i in range(blocks):
            for j in range(4):
                pairs.append((4 * i + j, 4 * (i ^ 8 if j % 2 else i) + (j ^ 2)))
        return lax.ppermute(array, ("seq", "head"), pairs)

    order = (2, 3, 1, 0)
    groups = [2 * (h ^ bit) + part for bit in order for part in range(2)]
    info = jnp.stack([s, *groups]).astype(jnp.int32)

    l1, to_near, to_far = pool(keys, values)
    near = permute(to_near, lambda i: i ^ 1)
    out_weight, l1 = lax.optimization_barrier((out_weight, l1))
    w_far = cross(out_weight)
    w_near = swap(out_weight, 1)
    to_far, l3 = middle(to_near, near, to_far, blocks // 2)
    far = permute(to_far, lambda i: i + 1 if i % 2 else i - 1)
    farther = permute(to_far[BK:, :], lambda i: i + 2 if i % 2 else i - 2)
    peers = [[2 * i + parity for i in range(blocks // 2)] for parity in range(2)]
    l3 = lax.all_to_all(l3, "seq", 0, 0, axis_index_groups=peers)

    w_far, w_near, far = lax.optimization_barrier((w_far, w_near, far))
    w_cross = swap(w_far, 1)
    rows = (queries, keys, keys, keys, values, values, values)
    small = (l1, to_far, near, far, farther, l3)
    foreign = [swap(attend(total, part, 1, info, rows, small), 2) for part in range(2)]
    last = swap(attend(total, 2, 2, info, rows, small), 3)
    inside = swap(attend(total, 4, 2, info, rows, small), 1)
    own = attend(total, 6, 2, info, rows, small)

    inner = project([own, *foreign, inside], [out_weight, w_far, w_near], [], F32)
    return finish(last, w_cross, inner, [*foreign, last])


def solution(mesh):
    placed = (P("seq", "head"), P("seq", "head"), P("seq", "head"), P("head", None))
    return jax.shard_map(
        body, mesh=mesh, in_specs=placed, out_specs=P(("seq", "head"), None), check_vma=False
    )
```

```python
import functools

import jax
import jax.numpy as jnp
from jax import lax
from jax.experimental import pallas as pl
from jax.experimental.pallas import tpu as pltpu
from jax.sharding import PartitionSpec as P

HD = 128
HEADS = 4
WIDE = HEADS * HD
LOG2E = 1.4426950408889634
SCORE = HD**-0.5 * LOG2E
NEG = -1e30
F32 = jnp.float32
BF16 = jnp.bfloat16
POOL_VMEM, ATTEND_VMEM, PROJECT_VMEM = (mib * 1024 * 1024 for mib in (53, 51, 24))
CHUNKS = 4
PROJECT_COST = pl.CostEstimate(flops=20000000000, bytes_accessed=70000000, transcendentals=0)
ATTEND_COST = pl.CostEstimate(flops=20000000000, bytes_accessed=70000000, transcendentals=0)
SMALL = pl.CostEstimate(flops=1000, bytes_accessed=1000, transcendentals=0)

TK, TV, AK, AV, BK, BV = (16 * i for i in range(6))


def mean_rows(count, size, scale):
    rows = lax.broadcasted_iota(jnp.int32, (count, count * size), 0)
    cols = lax.broadcasted_iota(jnp.int32, (count, count * size), 1)
    return jnp.where(rows == cols // size, scale, 0.0).astype(BF16)


def pool_kernel(k_hbm, v_hbm, l1_ref, near_ref, far_ref, k_ref, v_ref, sems):
    odd = lax.axis_index("seq") % 2
    ones = mean_rows(16, 16, 1.0)
    chunk = k_ref.shape[0] // CHUNKS
    copies = []
    for i in range(CHUNKS):
        rows = pl.ds(chunk * i, chunk)
        for which, (hbm, ref) in enumerate(((k_hbm, k_ref), (v_hbm, v_ref))):
            copy = pltpu.make_async_copy(hbm.at[rows, :], ref.at[rows, :], sems.at[which, i])
            copy.start()
            copies.append(copy)
    level2 = [[], []]
    for i in range(CHUNKS):
        for which, ref in enumerate((k_ref, v_ref)):
            copies[2 * i + which].wait()
            for at in range(chunk * i, chunk * (i + 1), 256):
                total = jnp.dot(ones, ref[at : at + 256, :], preferred_element_type=F32)
                l1_ref[which, at // 16 : at // 16 + 16, :] = (total * 0.0625).astype(BF16)
                level2[which].append(jnp.sum(total, axis=0, keepdims=True) * (1.0 / 256.0))

    last = k_ref.shape[0]
    low = [k_ref[0:16, :], v_ref[0:16, :], l1_ref[0, 0:16, :], l1_ref[1, 0:16, :]]
    high = [k_ref[last - 16 : last, :], v_ref[last - 16 : last, :]]
    high += [l1_ref[which, last // 16 - 16 : last // 16, :] for which in range(2)]
    for at, (below, above) in enumerate(zip(low, high)):
        rows = slice(16 * at, 16 * at + 16)
        near_ref[rows, :] = jnp.where(odd == 1, below, above)
        far_ref[rows, :] = jnp.where(odd == 1, above, below)
    row = lax.broadcasted_iota(jnp.int32, (16, WIDE), 0)
    for which, at in ((0, BK), (1, BV)):
        both = jnp.concatenate(level2[which] * 2, axis=0)
        near_ref[at : at + 16, :] = jnp.where(row // 8 == odd, both, 0.0).astype(BF16)


def pool(keys, values):
    rows = keys.shape[0]
    return pl.pallas_call(
        pool_kernel,
        in_specs=[
            pl.BlockSpec(memory_space=pltpu.HBM),
            pl.BlockSpec(memory_space=pltpu.HBM),
        ],
        out_specs=[pl.BlockSpec(memory_space=pltpu.VMEM)] * 3,
        scratch_shapes=[
            pltpu.VMEM((rows, WIDE), BF16),
            pltpu.VMEM((rows, WIDE), BF16),
            pltpu.SemaphoreType.DMA((2, CHUNKS)),
        ],
        out_shape=[
            jax.ShapeDtypeStruct((2, rows // 16, WIDE), BF16),
            jax.ShapeDtypeStruct((96, WIDE), BF16),
            jax.ShapeDtypeStruct((64, WIDE), BF16),
        ],
        cost_estimate=pl.CostEstimate(flops=4000000000, bytes_accessed=14000000, transcendentals=0),
        compiler_params=pltpu.CompilerParams(vmem_limit_bytes=POOL_VMEM),
        name="pool",
    )(keys, values)


def middle_kernel(own_ref, near_ref, far_ref, to_far_ref, l3_ref):
    to_far_ref[0:64, :] = far_ref[...]
    means = []
    for at in (BK, BV):
        rows = slice(at, at + 16)
        pair = own_ref[rows, :].astype(F32) + near_ref[rows, :].astype(F32)
        to_far_ref[rows, :] = pair.astype(BF16)
        mean = jnp.sum(pair, axis=0, keepdims=True) * 0.0625
        means += [mean[:, HD * head : HD * head + HD] for head in range(HEADS)]
    both = jnp.concatenate(means, axis=0).astype(BF16)
    l3_ref[...] = jnp.broadcast_to(both[None], l3_ref.shape)


def middle(own, near, far, copies):
    return pl.pallas_call(
        middle_kernel,
        out_shape=[
            jax.ShapeDtypeStruct((96, WIDE), BF16),
            jax.ShapeDtypeStruct((copies, 2 * HEADS, HD), BF16),
        ],
        cost_estimate=pl.CostEstimate(flops=1000000000, bytes_accessed=3500000, transcendentals=0),
        compiler_params=pltpu.CompilerParams(vmem_limit_bytes=4 * 1024 * 1024),
        name="middle",
    )(own, near, far)


def attend_kernel(
    total, base, info, q_ref, k_ref, kp_ref, kn_ref, v_ref, vp_ref, vn_ref, far_ref, l1_ref, mid_ref,
    near_ref, farther_ref, l3_ref, out_ref, kx, vx, l1x, sk, sv,
):
    step = pl.program_id(0)
    block = info[0]
    group = info[1 + base + step]
    odd = block % 2
    last_group = 2048 // 256 - 1

    @pl.when(step == 0)
    def _():
        for which, at in ((0, AK), (1, AV)):
            near, far = near_ref[at : at + 16, :], far_ref[at : at + 16, :]
            l1x[which, 0:16, :] = jnp.where(odd == 1, near, far)
            l1x[which, 16:144, :] = l1_ref[which]
            l1x[which, 144:160, :] = jnp.where(odd == 1, far, near)
        parts = 2 * HEADS * l3_ref.shape[0]
        wanted = lax.broadcasted_iota(jnp.int32, (parts, parts), 0)
        given = lax.broadcasted_iota(jnp.int32, (parts, parts), 1)
        pick = given == 2 * HEADS * (wanted % 32) + wanted // 32
        level3 = jnp.dot(
            jnp.where(pick, 1.0, 0.0).astype(BF16),
            l3_ref[...].reshape(parts, HD),
            preferred_element_type=F32,
        ).astype(BF16)
        for scratch, at, which in ((sk, BK, 0), (sv, BV, 1)):
            scratch[48:64, :] = mid_ref[at : at + 16, :]
            scratch[64:80, :] = far_ref[at : at + 16, :]
            scratch[80:96, :] = farther_ref[at - BK : at - BK + 16, :]
            for head in range(HEADS):
                first = 32 * (HEADS * which + head)
                scratch[96:128, HD * head : HD * head + HD] = level3[first : first + 32, :]
        zeros = jnp.zeros((32, WIDE), BF16)
        kx[288:320, :] = zeros
        vx[288:320, :] = zeros

    for scratch, main, before, after, at in (
        (kx, k_ref, kp_ref, kn_ref, TK),
        (vx, v_ref, vp_ref, vn_ref, TV),
    ):
        near, far = near_ref[at : at + 16, :], far_ref[at : at + 16, :]
        low = jnp.where(odd == 1, near, far)
        high = jnp.where(odd == 1, far, near)
        scratch[0:16, :] = jnp.where(group == 0, low, before[...])
        scratch[16:272, :] = main[...]
        scratch[272:288, :] = jnp.where(group == last_group, high, after[...])
    window = pl.ds(pl.multiple_of(16 * group, 16), 48)
    sk[0:48, :] = l1x[0, window, :]
    sv[0:48, :] = l1x[1, window, :]

    c = 8 * block + group
    e = block // 2
    col = lax.broadcasted_iota(jnp.int32, (64, 128), 1)
    fine = lax.broadcasted_iota(jnp.int32, (64, 128), 0) // 16
    tile = col // 16
    beside = jnp.where(odd == 0, e - 1, e + 1)
    across = jnp.where(odd == 0, e + 1, e - 1)
    m = 16 * jnp.where(tile == 3, e, jnp.where(tile == 4, beside, across)) + col % 16
    term2 = jnp.where((m >= 0) & (m < total // 256) & (jnp.abs(m - c) > 1), 0.0, NEG)
    term3 = jnp.where(jnp.abs(col - 96 - e) > 1, 0.0, NEG)
    j = 16 * (c - 1) + col
    term1 = jnp.where((j >= 0) & (j < total // 16), 0.0, NEG)
    shared = jnp.where(col < 48, term1, jnp.where(col < 96, term2, term3))

    pairs = [(part, head) for part in range(4) for head in range(HEADS)]
    cols = [slice(HD * head, HD * head + HD) for head in range(HEADS)]
    rows = [slice(64 * part, 64 * part + 64) for part in range(4)]
    near_rows = [slice(64 * part, 64 * part + 128) for part in range(4)]
    biases = []
    for part in range(4):
        token = 256 * c + 64 * part - 16 + col
        ok = (jnp.abs(tile - 1 - fine) <= 1) & (token >= 0) & (token < total)
        own = (col < 48) & (jnp.abs(col - 16 - 4 * part - fine) <= 1)
        terms = [jnp.where(ok, 0.0, NEG), jnp.where(own, NEG, shared)]
        biases.append(jnp.concatenate(terms, axis=1).astype(F32))
    scores, weights, sums = [], [], []
    for part, head in pairs:
        key_rows = jnp.concatenate([kx[near_rows[part], cols[head]], sk[:, cols[head]]], axis=0)
        raw = lax.dot_general(
            q_ref[rows[part], cols[head]], key_rows, (((1,), (1,)), ((), ())), preferred_element_type=F32
        )
        scores.append(raw * SCORE + biases[part])
    peaks = [jnp.max(score, axis=1, keepdims=True) for score in scores]
    for score, peak in zip(scores, peaks):
        expo = jnp.exp2(score - peak)
        sums.append(jnp.sum(expo, axis=1, keepdims=True))
        weights.append(expo.astype(BF16))
    summed = []
    for (part, head), weight in zip(pairs, weights):
        value_rows = jnp.concatenate([vx[near_rows[part], cols[head]], sv[:, cols[head]]], axis=0)
        summed.append(jnp.dot(weight, value_rows, preferred_element_type=F32))
    for (part, head), value, sum_ in zip(pairs, summed, sums):
        out_ref[rows[part], cols[head]] = (value * (1.0 / sum_)).astype(BF16)


def windows(base):
    def main(i, s):
        return (s[1 + base + i], 0)

    def before(i, s):
        return (jnp.maximum(16 * s[1 + base + i] - 1, 0), 0)

    def after(i, s):
        return (jnp.minimum(16 * s[1 + base + i] + 16, 127), 0)

    wide, thin_low, thin_high = (
        pl.BlockSpec((256, WIDE), main),
        pl.BlockSpec((16, WIDE), before),
        pl.BlockSpec((16, WIDE), after),
    )
    return [wide, wide, thin_low, thin_high, wide, thin_low, thin_high]


def attend(total, base, steps, info, rows, small):
    def whole(array):
        return pl.BlockSpec(array.shape, lambda i, s: (0,) * array.ndim)

    return pl.pallas_call(
        functools.partial(attend_kernel, total, base),
        grid_spec=pltpu.PrefetchScalarGridSpec(
            num_scalar_prefetch=1,
            grid=(steps,),
            in_specs=windows(base) + [whole(array) for array in small],
            out_specs=pl.BlockSpec((256, WIDE), lambda i, s: (i, 0)),
            scratch_shapes=[
                pltpu.VMEM((320, WIDE), BF16),
                pltpu.VMEM((320, WIDE), BF16),
                pltpu.VMEM((2, 160, WIDE), BF16),
                pltpu.VMEM((128, WIDE), BF16),
                pltpu.VMEM((128, WIDE), BF16),
            ],
        ),
        out_shape=jax.ShapeDtypeStruct((256 * steps, WIDE), BF16),
        cost_estimate=ATTEND_COST,
        compiler_params=pltpu.CompilerParams(vmem_limit_bytes=ATTEND_VMEM),
        name="attend",
    )(info, *rows, *small)


def project_kernel(n, *refs):
    weights, attended, out_ref, tiles, sems = refs[:n], refs[n:-3], refs[-3], refs[-2], refs[-1]
    count, depth, width = tiles.shape
    copies = []
    for i in range(count):
        for j, w in enumerate(weights):
            target = tiles.at[i, pl.ds(j * depth // n, depth // n), :]
            copies.append(pltpu.make_async_copy(w.at[:, pl.ds(i * width, width)], target, sems.at[i, j]))
            copies[-1].start()
    whole, halves = [], []
    for a in attended:
        if a.shape[0] == out_ref.shape[0]:
            whole.append(a[...])
        else:
            halves.append(a[...])
            if len(halves) == 2:
                whole.append(jnp.concatenate(halves, axis=0))
                halves = []
    left = jnp.concatenate(whole, axis=1)
    for i in range(count):
        for copy in copies[n * i : n * i + n]:
            copy.wait()
        out_ref[:, width * i : width * i + width] = jnp.dot(left, tiles[i], preferred_element_type=F32)


def project(attended, weights):
    rows, columns = attended[0].shape[0], weights[0].shape[1]
    depth = sum(w.shape[0] for w in weights)
    tiles = 4
    return pl.pallas_call(
        functools.partial(project_kernel, len(weights)),
        in_specs=[pl.BlockSpec(memory_space=pl.ANY) for _ in weights]
        + [pl.BlockSpec(memory_space=pltpu.VMEM) for _ in attended],
        out_specs=pl.BlockSpec(memory_space=pltpu.VMEM),
        scratch_shapes=[
            pltpu.VMEM((tiles, depth, columns // tiles), BF16),
            pltpu.SemaphoreType.DMA((tiles, len(weights))),
        ],
        out_shape=jax.ShapeDtypeStruct((rows, columns), F32),
        cost_estimate=PROJECT_COST,
        compiler_params=pltpu.CompilerParams(vmem_limit_bytes=PROJECT_VMEM),
        name="project",
    )(*weights, *attended)


def finish_kernel(ahead, *refs):
    before, weight, attended, out, tiles, sems = refs[ahead:]
    width = tiles.shape[2]
    copies = []
    for i in range(tiles.shape[0]):
        cols = slice(width * i, width * i + width)
        total = jnp.dot(attended[...], weight[:, cols], preferred_element_type=F32) + before[:, cols]
        tiles[i] = total.astype(BF16)
        copies.append(pltpu.make_async_copy(tiles.at[i], out.at[:, pl.ds(width * i, width)], sems.at[i]))
        copies[-1].start()
    for copy in copies:
        copy.wait()


def finish(attended, weight, before, ahead):
    rows, columns = before.shape
    tiles = 4
    return pl.pallas_call(
        functools.partial(finish_kernel, len(ahead)),
        in_specs=[pl.BlockSpec(memory_space=pl.ANY) for _ in ahead]
        + [pl.BlockSpec(memory_space=pltpu.VMEM)] * 3,
        out_specs=pl.BlockSpec(memory_space=pl.ANY),
        scratch_shapes=[
            pltpu.VMEM((tiles, rows, columns // tiles), BF16),
            pltpu.SemaphoreType.DMA((tiles,)),
        ],
        out_shape=jax.ShapeDtypeStruct((rows, columns), BF16),
        cost_estimate=PROJECT_COST,
        compiler_params=pltpu.CompilerParams(vmem_limit_bytes=PROJECT_VMEM),
        name="finish",
    )(*ahead, before, weight, attended)


def body(queries, keys, values, out_weight):
    blocks = lax.axis_size("seq")
    total = queries.shape[0] * blocks
    s = lax.axis_index("seq")
    h = lax.axis_index("head")

    def permute(array, move):
        return lax.ppermute(array, "seq", [(i, move(i) % blocks) for i in range(blocks)])

    def swap(array, bit):
        return lax.ppermute(array, "head", [(i, i ^ bit) for i in range(4)])

    def cross(array):
        pairs = []
        for i in range(blocks):
            for j in range(4):
                pairs.append((4 * i + j, 4 * (i ^ 8 if j % 2 else i) + (j ^ 2)))
        return lax.ppermute(array, ("seq", "head"), pairs)

    order = (2, 3, 1, 0)
    groups = [2 * (h ^ bit) + part for bit in order for part in range(2)]
    info = jnp.stack([s, *groups]).astype(jnp.int32)

    l1, to_near, to_far = pool(keys, values)
    near = permute(to_near, lambda i: i ^ 1)
    out_weight, l1 = lax.optimization_barrier((out_weight, l1))
    w_far = cross(out_weight)
    w_near = swap(out_weight, 1)
    to_far, l3 = middle(to_near, near, to_far, blocks // 2)
    far = permute(to_far, lambda i: i + 1 if i % 2 else i - 1)
    farther = permute(to_far[BK:, :], lambda i: i + 2 if i % 2 else i - 2)
    peers = [[2 * i + parity for i in range(blocks // 2)] for parity in range(2)]
    l3 = lax.all_to_all(l3, "seq", 0, 0, axis_index_groups=peers)

    w_far, w_near, far = lax.optimization_barrier((w_far, w_near, far))
    w_cross = swap(w_far, 1)
    rows = (queries, keys, keys, keys, values, values, values)
    small = (far, l1, to_far, near, farther, l3)
    foreign = [swap(attend(total, part, 1, info, rows, small), 2) for part in range(2)]
    last = swap(attend(total, 2, 2, info, rows, small), 3)
    inside = swap(attend(total, 4, 2, info, rows, small), 1)
    own = attend(total, 6, 2, info, rows, small)

    inner = project([own, *foreign, inside], [out_weight, w_far, w_near])
    return finish(last, w_cross, inner, [*foreign, last])


def solution(mesh):
    placed = (P("seq", "head"), P("seq", "head"), P("seq", "head"), P("head", None))
    return jax.shard_map(
        body, mesh=mesh, in_specs=placed, out_specs=P(("seq", "head"), None), check_vma=False
    )
```
